128 devices in a mesh: ctx: 8 (over z, y_hi), exp: 16 (over x, y_lo, core).
Axes of the slice: x: 4, y: 4 (y_hi: 2, y_lo: 2; y = y_hi * 2 + y_lo), z: 4, core: 2. Of those that a mesh axis runs over, the one named last changes fastest.
Arguments:
- q_nope: bfloat16 [2048, 16384], P('ctx', 'exp'), may hold values from -6 to 6
- q_rope: bfloat16 [2048, 8192], P('ctx', 'exp'), may hold values from -24 to 24
- kv_latent: bfloat16 [2048, 512], P('ctx'), may hold values from -6 to 6
- key_rope: bfloat16 [2048, 64], P('ctx'), may hold values from -6 to 6
- w_uk: bfloat16 [128, 128, 512], P('exp'), may hold values from -0.5 to 0.5
- w_uv: bfloat16 [128, 512, 128], P('exp'), may hold values from -1 to 1
- w_out: bfloat16 [16384, 7168], P('exp', 'ctx'), may hold values from -0.09375 to 0.09375
- w_gate: bfloat16 [16, 7168, 2048], P('exp', 'ctx'), may hold values from -0.0625 to 0.0625
- w_up: bfloat16 [16, 7168, 2048], P('exp', 'ctx'), may hold values from -0.0625 to 0.0625
- w_down: bfloat16 [16, 2048, 7168], P('exp', None, 'ctx'), may hold values from -0.125 to 0.125
- route_ids: int32 [2048, 4], P('exp'), may hold values from 0 to 15, all different within a row; in each aligned block of 128 rows (0 to 127, 128 to 255, ...) at most 48 rows name the same one
- route_gates: bfloat16 [2048, 4], P('exp'), may hold values from 0.19921875 to 1
Outputs:
- attn_out: bfloat16 [2048, 7168], P('exp', 'ctx')
- moe_out: bfloat16 [2048, 7168], P('exp', 'ctx')
The draws below stay inside these ranges and needn't reach their ends.
Inputs may be any that keep to these rules, and one draw needn't show every extreme that they name: `route_ids`: each row names 4 different experts. In each aligned block of 128 rows no expert is named by more than 48 rows, and in some block one expert is named by exactly 48 rows.
All inputs are finite; a program needn't handle non-finite values.
Results may differ from the reference program's by a relative error of at most 0.035.
Values may be sent and summed in bfloat16 or wider, within the bound.
No kernel may reach another device: no remote copies, remote signals or barrier semaphores. Data moves between devices by JAX's collectives and lax.ppermute only.
A program may use at most 128 MiB of HBM per device.

```python
import math
from functools import partial
import jax
import jax.numpy as jnp
import numpy as np
from jax import lax

D = 7168
HEADS = 128
NOPE = 128
ROPE = 64
VHEAD = 128
LATENT = 512
FF = 2048
TOP = 4
SEQ = 2048
ROWS_EXP = 128
EXPERTS = 16
CAP = 48
N_CTX = 8
N_EXP = 16


def draw_q_nope(key, part):
    key = jax.random.fold_in(key, 1)
    return jnp.clip(jax.random.normal(key, (SEQ, HEADS * NOPE), jnp.float32), -6.0, 6.0).astype(jnp.bfloat16)


def draw_key_rope(key, part):
    key = jax.random.fold_in(key, 2)
    values = jnp.clip(jax.random.normal(key, (SEQ, ROPE), jnp.float32), -6.0, 6.0)
    return values.astype(jnp.bfloat16)


def draw_q_rope(key, part):
    key = jax.random.fold_in(key, 3)
    values = jnp.clip(jax.random.normal(key, (SEQ, HEADS * ROPE), jnp.float32), -6.0, 6.0)
    return values.astype(jnp.bfloat16)


def block_scale(own_key, shape, shards, least, top_value):
    def one(axis_at, blocks):
        steps = jax.random.uniform(jax.random.fold_in(jax.random.fold_in(own_key, 6), axis_at), (blocks,), jnp.float32, least / len(shards), top_value / len(shards))
        return jnp.repeat(jnp.exp(steps), shape[axis_at] // blocks).reshape((-1,) + (1,) * (len(shape) - axis_at - 1))

    loudness = one(*shards[0])
    for cut in shards[1:]:
        loudness = loudness * one(*cut)
    return loudness


def assign_block(stream_key, own, number, rows, number_of, top, reach, slope):
    order = jax.random.permutation(stream_key, number_of)
    heavy_load, usual = shares(number_of, rows * top, reach, slope, True), shares(number_of, rows * top, reach, slope, False)
    places = jnp.arange(number_of)

    def named(tallies, turn):
        used = int((tallies > 0).sum())
        fixed = max(1, used // 4)
        moved = fixed + (places - fixed + turn * (used - fixed)) % max(1, number_of - fixed)
        return jnp.zeros((number_of,), jnp.int32).at[order[jnp.where(places < fixed, places, moved)]].set(jnp.asarray(tallies, jnp.int32))

    tallies = jnp.where(number % 4 == 0, named(heavy_load, number // 4), named(usual, number - number // 4 - 1))
    mixed = jax.random.permutation(jax.random.fold_in(own, 3), number_of)
    source_of, receiver = mixed[0:number_of // 2 * 2:2], mixed[1:number_of // 2 * 2:2]
    slack = jnp.minimum(tallies[source_of] - 1, reach - tallies[receiver]) // 2
    slack = jnp.where((source_of == order[0]) | (receiver == order[0]) | (tallies[receiver] == 0), 0, jnp.maximum(slack, 0))
    moved = jax.random.randint(jax.random.fold_in(own, 4), (number_of // 2,), 0, 1 << 20) % (slack + 1)
    tallies = tallies.at[source_of].add(-moved).at[receiver].add(moved)
    labels = jnp.searchsorted(jnp.cumsum(tallies), jnp.arange(rows * top), side="right").astype(jnp.int32)
    listing = labels.reshape(top, rows).T
    listing = listing[jax.random.permutation(jax.random.fold_in(own, 1), rows)]
    turn = jax.random.randint(jax.random.fold_in(own, 2), (rows, 1), 0, top)
    return jnp.take_along_axis(listing, (jnp.arange(top)[None, :] + turn) % top, axis=1)


def shares(count, total, reach, lean, full):
    weights = [(1 << 20) // math.isqrt(standing ** lean) + 1 for standing in range(1, count + 1)]
    largest = reach if full else min(reach, max(-(-total // count), total * weights[0] // sum(weights)))
    least = 1 if total - largest >= count - 1 else 0
    given, surplus = [largest] + [least] * (count - 1), total - largest - least * (count - 1)
    while surplus > 0:
        movable = [i for i in range(1, count) if given[i] < largest] or [i for i in range(1, count) if given[i] < reach]
        mass, budget = sum([weights[i] for i in movable]), surplus
        for i in movable:
            extra = min(reach - given[i], max(1, budget * weights[i] // mass), surplus)
            given[i] = given[i] + extra
            surplus = surplus - extra
    return np.array(given)


def gaussian(stream_key, extent, scale, limit, pieces=(), held_as=jnp.bfloat16):
    level = block_scale(stream_key, extent, pieces, -0.22, 0.18) if pieces else 1.0
    array = jax.random.normal(stream_key, extent, jnp.float32) * scale * level
    return jnp.minimum(jnp.maximum(array, -limit), limit).astype(held_as)


def setup_inputs(seed: int = 0) -> dict:
    arg_keys = jax.random.split(jax.random.key(seed), 13)
    q_nope = draw_q_nope(jax.random.fold_in(arg_keys[12], 71), 0)
    q_rope = draw_q_rope(jax.random.fold_in(arg_keys[12], 71), 0)
    kv_latent = gaussian(arg_keys[2], (SEQ, LATENT), 1.0, 6.0, ((0, 8),))
    key_rope = draw_key_rope(jax.random.fold_in(arg_keys[12], 71), 0)
    w_uk = gaussian(arg_keys[4], (HEADS, NOPE, LATENT), NOPE ** -0.5, 0.5, ((0, 16),))
    w_uv = gaussian(arg_keys[5], (HEADS, LATENT, VHEAD), (LATENT // 16) ** -0.5, 1.0, ((0, 16),))
    w_out = gaussian(arg_keys[6], (HEADS * VHEAD, D), (HEADS * VHEAD // 4) ** -0.5, 0.09375, ((0, 16), (1, 8)))
    w_gate = gaussian(arg_keys[7], (EXPERTS, D, FF), D ** -0.5, 0.0625, ((0, 16), (1, 8)))
    w_up = gaussian(arg_keys[8], (EXPERTS, D, FF), D ** -0.5, 0.0625, ((0, 16), (1, 8)))
    w_down = gaussian(arg_keys[9], (EXPERTS, FF, D), FF ** -0.5, 0.125, ((0, 16), (2, 8)))
    route_ids_keys = jax.random.split(jax.random.fold_in(arg_keys[10], 1), SEQ // ROWS_EXP)
    route_ids_turns = jax.random.permutation(jax.random.fold_in(arg_keys[10], 3), SEQ // ROWS_EXP)
    route_ids = jax.vmap(lambda own, number: assign_block(jax.random.fold_in(arg_keys[10], 2), own, number, ROWS_EXP, EXPERTS, TOP, CAP, 2))(route_ids_keys, route_ids_turns).reshape((SEQ, TOP))
    route_gates = jnp.clip(0.19921875 + 0.80078125 * jax.random.uniform(arg_keys[11], (SEQ, TOP), jnp.float32) ** block_scale(arg_keys[11], (SEQ, TOP), ((0, 16),), -0.2, 0.2), 0.19921875, 1.0).astype(jnp.bfloat16)
    return dict(q_nope=q_nope, q_rope=q_rope, kv_latent=kv_latent, key_rope=key_rope, w_uk=w_uk, w_uv=w_uv, w_out=w_out, w_gate=w_gate, w_up=w_up, w_down=w_down, route_ids=route_ids, route_gates=route_gates)


def head_attention(inputs, kv_latent, key_rope):
    query_nope, query_rope, uk_matrix, uv_matrix = inputs
    query_latent = jnp.dot(query_nope, uk_matrix, preferred_element_type=jnp.float32).astype(jnp.bfloat16)
    scores = jnp.dot(query_latent, kv_latent.T, preferred_element_type=jnp.float32)
    scores = scores + jnp.dot(query_rope, key_rope.T, preferred_element_type=jnp.float32)
    scores = scores * (1.0 / math.sqrt(NOPE + ROPE))
    positions = jnp.arange(SEQ, dtype=jnp.int32)
    allowed = positions[None, :] <= positions[:, None]
    largest = lax.optimization_barrier(jnp.max(jnp.where(allowed, scores, -jnp.inf), axis=1, keepdims=True))
    exp_terms = jnp.where(allowed, jnp.exp(scores - largest), 0.0)
    totals = lax.optimization_barrier(jnp.sum(exp_terms, axis=1, keepdims=True))
    mixed = jnp.dot(exp_terms.astype(jnp.bfloat16), kv_latent, preferred_element_type=jnp.float32)
    latent_out = (mixed / totals).astype(jnp.bfloat16)
    return jnp.dot(latent_out, uv_matrix, preferred_element_type=jnp.float32).astype(jnp.bfloat16)

def expert_rows(inputs, tokens):
    row_index, gate_matrix, up_matrix, down_matrix = inputs
    block_cols = D // N_CTX
    chosen = tokens[row_index].astype(jnp.float32).reshape(-1, N_CTX, block_cols)
    gate_blocks = gate_matrix.astype(jnp.float32).reshape(N_CTX, block_cols, FF)
    up_blocks = up_matrix.astype(jnp.float32).reshape(N_CTX, block_cols, FF)
    gate_part = jnp.einsum('rcd,cdf->crf', chosen, gate_blocks, precision=lax.Precision.HIGHEST).astype(jnp.bfloat16)
    up_part = jnp.einsum('rcd,cdf->crf', chosen, up_blocks, precision=lax.Precision.HIGHEST).astype(jnp.bfloat16)
    gate_pre = lax.optimization_barrier(jnp.sum(gate_part.astype(jnp.float32), axis=0))
    up_pre = lax.optimization_barrier(jnp.sum(up_part.astype(jnp.float32), axis=0))
    hidden = (jax.nn.silu(gate_pre) * up_pre).astype(jnp.bfloat16)
    return jnp.dot(hidden, down_matrix, preferred_element_type=jnp.float32).astype(jnp.bfloat16)

def reference(q_nope, q_rope, kv_latent, key_rope, w_uk, w_uv, w_out, w_gate, w_up, w_down, route_ids, route_gates):
    nope_heads = q_nope.reshape(SEQ, HEADS, NOPE).transpose(1, 0, 2)
    rope_heads = q_rope.reshape(SEQ, HEADS, ROPE).transpose(1, 0, 2)
    head_out = lax.map(partial(head_attention, kv_latent=kv_latent, key_rope=key_rope), (nope_heads, rope_heads, w_uk, w_uv))
    head_flat = head_out.transpose(1, 0, 2).reshape(SEQ, HEADS * VHEAD)
    attn_out = jnp.dot(head_flat, w_out, preferred_element_type=jnp.float32).astype(jnp.bfloat16)
    flat_ids = route_ids.reshape(-1).astype(jnp.int32)
    onehot = (flat_ids[:, None] == jnp.arange(EXPERTS, dtype=jnp.int32)[None, :]).astype(jnp.int32)
    ranks = lax.optimization_barrier(jnp.sum((jnp.cumsum(onehot, axis=0) - onehot) * onehot, axis=1)).astype(jnp.int32)
    owners = jnp.repeat(jnp.arange(SEQ, dtype=jnp.int32), TOP)
    table = jnp.zeros((EXPERTS, N_EXP * CAP), jnp.int32).at[flat_ids, ranks].set(owners)
    outputs = lax.map(partial(expert_rows, tokens=attn_out), (table, w_gate, w_up, w_down))
    picked = outputs[flat_ids, ranks].reshape(SEQ, TOP, D)
    moe_sum = lax.optimization_barrier(jnp.sum(route_gates.astype(jnp.float32)[:, :, None] * picked.astype(jnp.float32), axis=1))
    return (attn_out, moe_sum.astype(jnp.bfloat16))
```

```python
import functools
import math

import jax
import jax.numpy as jnp
from jax import lax
from jax.experimental import pallas as pl
from jax.experimental.pallas import tpu as pltpu
from jax.sharding import PartitionSpec as P

BF = jnp.bfloat16
F32 = jnp.float32
NEG_FILL = -1e30
PIECE = 128

ZS = 4
AG_ORDER = ((0, 0), (-1, 0), (1, 0), (0, 1), (-1, 1), (1, 1), (2, 0), (2, 1))


def z_shift(array, step):
    perm = [(z * 2 + y, ((z + step) % ZS) * 2 + y) for z in range(ZS) for y in range(2)]
    return lax.ppermute(array, "ctx", perm)


def y_swap(array):
    return lax.ppermute(array, "ctx", [(i, i ^ 1) for i in range(2 * ZS)])


def core_swap(array):
    return lax.ppermute(array, "exp", [(e, e ^ 1) for e in range(16)])


def ctx_at(here, dz, dy):
    z, y = here // 2, here % 2
    return ((z + dz) % ZS) * 2 + (y + dy) % 2


def gather_blocks(own):
    half = own.shape[0] // 2
    up, down, side = z_shift(own, 1), z_shift(own, -1), y_swap(own)
    far = jnp.concatenate([z_shift(up[:half], 1), z_shift(down[half:], -1)], axis=0)
    side_up, side_down = z_shift(side, 1), z_shift(side, -1)
    return own, up, down, side, side_up, side_down, far, y_swap(far)


def add(*terms):
    return functools.reduce(jnp.add, [t.astype(F32) for t in terms])


def scatter_sum(part):
    far_side, up_side, down_side = part(2, 1), part(1, 1), part(-1, 1)
    got_far, got_up, got_down = y_swap(far_side), z_shift(up_side, 1), z_shift(down_side, -1)
    far = add(part(2, 0), got_far).astype(BF)
    side = add(part(0, 1), got_up, got_down).astype(BF)
    half = far.shape[0] // 2
    far_up, far_down = z_shift(far[:half], 1), z_shift(far[half:], -1)
    got_side = y_swap(side)
    up, down = part(1, 0), part(-1, 0)
    up = jnp.concatenate([add(up[:half], far_up).astype(BF), up[half:]], axis=0)
    down = jnp.concatenate([down[:half], add(down[half:], far_down).astype(BF)], axis=0)
    return add(part(0, 0), got_side, z_shift(up, 1), z_shift(down, -1))


def attention_kernel(where_ref, qn_ref, qr_ref, kv_ref, uk_ref, uv_ref, out_ref, *, scale):
    rows = qn_ref.shape[0]
    keys = kv_ref.shape[0]
    latent = uk_ref.shape[2]
    nope = uk_ref.shape[1]
    vhead = uv_ref.shape[2]
    lanes = lax.broadcasted_iota(jnp.int32, (rows, qr_ref.shape[1]), 1)
    rope = qr_ref.shape[1] // 2
    ahead = lax.broadcasted_iota(jnp.int32, (rows, PIECE), 0) - lax.broadcasted_iota(
        jnp.int32, (rows, PIECE), 1
    )
    for h in range(uk_ref.shape[0]):
        query = jnp.dot(
            qn_ref[:, h * nope : (h + 1) * nope], uk_ref[h], preferred_element_type=F32
        ).astype(BF)
        mine = (lanes >= h * rope) & (lanes < (h + 1) * rope)
        turned = jnp.where(mine, qr_ref[...], jnp.zeros((), BF))
        query = jnp.concatenate([query, turned], axis=1)
        scores = lax.dot_general(
            query, kv_ref[...], (((1,), (1,)), ((), ())), preferred_element_type=F32
        )
        scores = jnp.concatenate(
            [
                jnp.where(ahead >= where_ref[p], scores[:, p * PIECE : (p + 1) * PIECE], NEG_FILL)
                for p in range(keys // PIECE)
            ],
            axis=1,
        )
        largest = jnp.max(scores, axis=1, keepdims=True)
        terms = jnp.exp2((scores - largest) * (scale * math.log2(math.e)))
        total = jnp.sum(terms, axis=1, keepdims=True)
        mixed = jnp.dot(terms.astype(BF), kv_ref[:, :latent], preferred_element_type=F32)
        mixed = (mixed / total).astype(BF)
        out_ref[:, h * vhead : (h + 1) * vhead] = jnp.dot(
            mixed, uv_ref[h], preferred_element_type=F32
        ).astype(BF)


def attention(where, q_nope, q_rope, keys, w_uk, w_uv):
    rows = q_nope.shape[0]
    heads, nope, latent = w_uk.shape
    vhead = w_uv.shape[2]
    rope = q_rope.shape[1] // heads
    kernel = functools.partial(attention_kernel, scale=1.0 / math.sqrt(nope + rope))
    pair = 2
    return pl.pallas_call(
        kernel,
        grid_spec=pltpu.PrefetchScalarGridSpec(
            num_scalar_prefetch=1,
            grid=(heads // pair,),
            in_specs=[
                pl.BlockSpec((rows, pair * nope), lambda i, w: (0, i)),
                pl.BlockSpec((rows, pair * rope), lambda i, w: (0, i)),
                pl.BlockSpec(keys.shape, lambda i, w: (0, 0)),
                pl.BlockSpec((pair, nope, latent), lambda i, w: (i, 0, 0)),
                pl.BlockSpec((pair, latent, vhead), lambda i, w: (i, 0, 0)),
            ],
            out_specs=pl.BlockSpec((rows, pair * vhead), lambda i, w: (0, i)),
        ),
        out_shape=jax.ShapeDtypeStruct((rows, heads * vhead), BF),
        compiler_params=pltpu.CompilerParams(vmem_limit_bytes=40 * 2**20),
        cost_estimate=pl.CostEstimate(
            flops=2 * rows * heads * keys.shape[0] * (keys.shape[1] + latent),
            bytes_accessed=2 * (keys.size + 2 * q_nope.size + q_rope.size + w_uk.size + w_uv.size),
            transcendentals=rows * heads * keys.shape[0],
        ),
    )(where, q_nope, q_rope, keys, w_uk, w_uv)


def local(
    q_nope,
    q_rope,
    kv_latent,
    key_rope,
    w_uk,
    w_uv,
    w_out,
    w_gate,
    w_up,
    w_down,
    route_ids,
    route_gates,
):
    tok_rows = q_nope.shape[0]
    ctx_here = lax.axis_index("ctx")
    core = lax.axis_index("exp") % 2
    ctx_size = lax.axis_size("ctx")
    order = [ctx_at(ctx_here, dz, dy) for dz, dy in AG_ORDER]

    key_rows = jnp.concatenate([kv_latent, key_rope, key_rope], axis=1)
    half_rows = tok_rows // 2
    blocks = gather_blocks(lax.dynamic_slice_in_dim(key_rows, core * half_rows, half_rows, 0))
    pieces, starts = [key_rows], [ctx_here * tok_rows, ctx_here * tok_rows + half_rows]
    for block, source in zip(blocks[1:], order[1:], strict=True):
        pieces += [block, core_swap(block)]
        starts += [
            source * tok_rows + core * half_rows,
            source * tok_rows + (1 - core) * half_rows,
        ]
    where = jnp.stack(starts) - ctx_here * tok_rows
    head_out = attention(where, q_nope, q_rope, jnp.concatenate(pieces, axis=0), w_uk, w_uv)

    sums = [
        jnp.dot(block, w_out, preferred_element_type=F32).astype(BF)
        for block in gather_blocks(head_out)
    ]
    sums = jnp.stack(sums).reshape(ctx_size, 2, half_rows, w_out.shape[1])
    inverse = jnp.zeros((ctx_size,), jnp.int32).at[jnp.stack(order)].set(
        jnp.arange(ctx_size, dtype=jnp.int32)
    )
    other = core_swap(lax.dynamic_index_in_dim(sums, 1 - core, 1, False))
    pair_sum = add(lax.dynamic_index_in_dim(sums, core, 1, False), other).astype(BF)
    pair_sum = jnp.take(pair_sum, inverse, axis=0)
    same_core = [[2 * i + c for i in range(8)] for c in range(2)]
    attn_out = (
        lax.all_to_all(pair_sum, "exp", 0, 0, tiled=True, axis_index_groups=same_core)
        .astype(F32)
        .sum(0)
        .astype(BF)
    )

    out_rows = attn_out.shape[0]
    feature_cols = attn_out.shape[1]
    top_count = route_ids.shape[1]
    expert_count = lax.axis_size("exp") * w_gate.shape[0]
    capacity = 3 * out_rows * top_count // (2 * expert_count)
    slot_total = expert_count * capacity
    flat_ids = route_ids.reshape(-1)
    onehot = (flat_ids[:, None] == jnp.arange(expert_count, dtype=jnp.int32)[None, :]).astype(
        jnp.int32
    )
    earlier = jnp.cumsum(onehot, axis=0) - onehot
    slot_ids = jnp.sum(earlier * onehot, axis=1)
    targets = (flat_ids * capacity + slot_ids).reshape(out_rows, top_count)
    slot_range = jnp.arange(slot_total, dtype=jnp.int32)
    hits = targets[:, :, None] == slot_range[None, None, :]
    placing = jnp.sum(hits.astype(F32), axis=1).astype(BF).T
    weighting = jnp.sum(jnp.where(hits, route_gates[:, :, None], jnp.zeros((), BF)), axis=1)
    send_rows = jnp.dot(placing, attn_out, preferred_element_type=F32).astype(BF)
    send_rows = send_rows.reshape(expert_count, capacity, feature_cols)
    arrived = lax.all_to_all(send_rows, "exp", split_axis=0, concat_axis=0, tiled=True)
    flat_rows = arrived.reshape(slot_total, feature_cols)

    hidden_cols = w_gate.shape[2] // ctx_size

    def part(dz, dy):
        first = ctx_at(ctx_here, dz, dy) * hidden_cols
        both = jnp.concatenate(
            [lax.dynamic_slice_in_dim(w[0], first, hidden_cols, 1) for w in (w_gate, w_up)], axis=1
        )
        return jnp.dot(flat_rows, both, preferred_element_type=F32).astype(BF)

    pre = scatter_sum(part)
    hidden = (jax.nn.silu(pre[:, :hidden_cols]) * pre[:, hidden_cols:]).astype(BF)
    all_hidden = jnp.concatenate(gather_blocks(hidden), axis=1)
    down_rows = jnp.concatenate(
        [lax.dynamic_slice_in_dim(w_down[0], i * hidden_cols, hidden_cols, 0) for i in order], axis=0
    )
    expert_out = jnp.dot(all_hidden, down_rows, preferred_element_type=F32).astype(BF)
    expert_out = expert_out.reshape(expert_count, capacity, feature_cols)
    returned = lax.all_to_all(expert_out, "exp", split_axis=0, concat_axis=0, tiled=True)
    moe_out = jnp.dot(
        weighting, returned.reshape(slot_total, feature_cols), preferred_element_type=F32
    ).astype(BF)
    return (attn_out, moe_out)


def solution(mesh):
    placed = (
        P("ctx", "exp"),
        P("ctx", "exp"),
        P("ctx", None),
        P("ctx", None),
        P("exp", None, None),
        P("exp", None, None),
        P("exp", "ctx"),
        P("exp", "ctx", None),
        P("exp", "ctx", None),
        P("exp", None, "ctx"),
        P("exp", None),
        P("exp", None),
    )
    return jax.shard_map(
        local,
        mesh=mesh,
        in_specs=placed,
        out_specs=(P("exp", "ctx"), P("exp", "ctx")),
        check_vma=False,
    )
```

```python
import functools
import math

import jax
import jax.numpy as jnp
from jax import lax
from jax.experimental import pallas as pl
from jax.experimental.pallas import tpu as pltpu
from jax.sharding import PartitionSpec as P

BF = jnp.bfloat16
F32 = jnp.float32
NEG_FILL = -1e30
PIECE = 128

ZS = 4
AG_ORDER = ((0, 0), (-1, 0), (1, 0), (0, 1), (-1, 1), (1, 1), (2, 0), (2, 1))


def z_shift(array, step):
    perm = [(z * 2 + y, ((z + step) % ZS) * 2 + y) for z in range(ZS) for y in range(2)]
    return lax.ppermute(array, "ctx", perm)


def y_swap(array):
    return lax.ppermute(array, "ctx", [(i, i ^ 1) for i in range(2 * ZS)])


def core_swap(array):
    return lax.ppermute(array, "exp", [(e, e ^ 1) for e in range(16)])


def ctx_at(here, dz, dy):
    z, y = here // 2, here % 2
    return ((z + dz) % ZS) * 2 + (y + dy) % 2


def first_blocks(own):
    return own, z_shift(own, 1), z_shift(own, -1), y_swap(own)


def gather_blocks(own):
    return other_blocks(first_blocks(own))


def other_blocks(blocks):
    own, up, down, side = blocks
    half = own.shape[0] // 2
    far = jnp.concatenate([z_shift(up[:half], 1), z_shift(down[half:], -1)], axis=0)
    side_up, side_down = z_shift(side, 1), z_shift(side, -1)
    return own, up, down, side, side_up, side_down, far, y_swap(far)


def add(*terms):
    return functools.reduce(jnp.add, [t.astype(F32) for t in terms])


def scatter_sum(part):
    far_side, up_side, down_side = part(2, 1), part(1, 1), part(-1, 1)
    got_far, got_up, got_down = y_swap(far_side), z_shift(up_side, 1), z_shift(down_side, -1)
    far = add(part(2, 0), got_far).astype(BF)
    side = add(part(0, 1), got_up, got_down).astype(BF)
    half = far.shape[0] // 2
    far_up, far_down = z_shift(far[:half], 1), z_shift(far[half:], -1)
    got_side = y_swap(side)
    up, down = part(1, 0), part(-1, 0)
    up = jnp.concatenate([add(up[:half], far_up).astype(BF), up[half:]], axis=0)
    down = jnp.concatenate([down[:half], add(down[half:], far_down).astype(BF)], axis=0)
    return add(part(0, 0), got_side, z_shift(up, 1), z_shift(down, -1))


def attention_kernel(where_ref, qn_ref, qr_ref, uk_ref, uv_ref, *refs, scale):
    *piece_refs, out_ref, keys = refs
    rows = qn_ref.shape[0]
    heads, nope, latent = uk_ref.shape
    vhead = uv_ref.shape[2]
    rope = qr_ref.shape[1] // heads
    factor = scale * math.log2(math.e)

    @pl.when(pl.program_id(0) == 0)
    def _():
        at = 0
        for ref in piece_refs:
            keys[at : at + ref.shape[0], :] = ref[...]
            at += ref.shape[0]

    lanes = lax.broadcasted_iota(jnp.int32, (rows, heads * rope), 1)
    ahead = lax.broadcasted_iota(jnp.int32, (rows, PIECE), 0) - lax.broadcasted_iota(
        jnp.int32, (rows, PIECE), 1
    )
    for h in range(heads):
        plain = jnp.dot(
            qn_ref[:, h * nope : (h + 1) * nope], uk_ref[h], preferred_element_type=F32
        ).astype(BF)
        mine = (lanes >= h * rope) & (lanes < (h + 1) * rope)
        turned = jnp.where(mine, qr_ref[...], jnp.zeros((), BF))
        scores = lax.dot_general(
            jnp.concatenate([plain, turned], axis=1),
            keys[...],
            (((1,), (1,)), ((), ())),
            preferred_element_type=F32,
        )
        scores = jnp.concatenate(
            [
                jnp.where(ahead >= where_ref[p], scores[:, p * PIECE : (p + 1) * PIECE], NEG_FILL)
                for p in range(keys.shape[0] // PIECE)
            ],
            axis=1,
        )
        largest = jnp.max(scores, axis=1, keepdims=True)
        terms = jnp.exp2((scores - largest) * factor)
        total = jnp.sum(terms, axis=1, keepdims=True)
        mixed = jnp.dot(terms.astype(BF), keys[:, :latent], preferred_element_type=F32)
        mixed = (mixed / total).astype(BF)
        out_ref[:, h * vhead : (h + 1) * vhead] = jnp.dot(
            mixed, uv_ref[h], preferred_element_type=F32
        ).astype(BF)


def attention(where, q_nope, q_rope, pieces, w_uk, w_uv):
    rows = q_nope.shape[0]
    heads, nope, latent = w_uk.shape
    vhead = w_uv.shape[2]
    rope = q_rope.shape[1] // heads
    pair = 2
    key_count = sum(p.shape[0] for p in pieces)
    width = pieces[0].shape[1]
    return pl.pallas_call(
        functools.partial(attention_kernel, scale=1.0 / math.sqrt(nope + rope)),
        grid_spec=pltpu.PrefetchScalarGridSpec(
            num_scalar_prefetch=1,
            grid=(heads // pair,),
            in_specs=[
                pl.BlockSpec((rows, pair * nope), lambda i, w: (0, i)),
                pl.BlockSpec((rows, pair * rope), lambda i, w: (0, i)),
                pl.BlockSpec((pair, nope, latent), lambda i, w: (i, 0, 0)),
                pl.BlockSpec((pair, latent, vhead), lambda i, w: (i, 0, 0)),
            ]
            + [pl.BlockSpec(p.shape, lambda i, w: (0, 0)) for p in pieces],
            out_specs=pl.BlockSpec((rows, pair * vhead), lambda i, w: (0, i)),
            scratch_shapes=[pltpu.VMEM((key_count, width), BF)],
        ),
        out_shape=jax.ShapeDtypeStruct((rows, heads * vhead), BF),
        compiler_params=pltpu.CompilerParams(vmem_limit_bytes=40 * 2**20),
        cost_estimate=pl.CostEstimate(
            flops=2 * rows * heads * key_count * (width + latent),
            bytes_accessed=2 * (key_count * width + 2 * q_nope.size),
            transcendentals=rows * heads * key_count,
        ),
    )(where, q_nope, q_rope, w_uk, w_uv, *pieces)


def project_kernel(place_ref, core_ref, w_ref, *refs):
    *block_refs, mine_ref, other_ref, weights, blocks, sem = refs
    rows = block_refs[0].shape[0]
    copies = [pltpu.make_async_copy(w_ref, weights, sem.at[len(block_refs)])]
    for n, ref in enumerate(block_refs):
        copies.append(pltpu.make_async_copy(ref, blocks.at[pl.ds(n * rows, rows)], sem.at[n]))
    for copy in copies:
        copy.start()
    for copy in copies:
        copy.wait()
    result = jnp.dot(blocks[...], weights[...], preferred_element_type=F32).astype(BF)
    even = core_ref[0] == 0
    for b in range(len(block_refs)):
        low = result[b * rows : b * rows + rows // 2]
        high = result[b * rows + rows // 2 : (b + 1) * rows]
        mine_ref[place_ref[b]] = jnp.where(even, low, high)
        other_ref[place_ref[b]] = jnp.where(even, high, low)


def project(places, core, w_out, blocks):
    rows, depth = blocks[0].shape
    columns = w_out.shape[1]
    shape = jax.ShapeDtypeStruct((len(blocks), rows // 2, columns), BF)
    vmem = pl.BlockSpec(memory_space=pltpu.VMEM)
    smem = pl.BlockSpec(memory_space=pltpu.SMEM)
    return pl.pallas_call(
        project_kernel,
        in_specs=[smem, smem] + [pl.BlockSpec(memory_space=pl.ANY)] * (1 + len(blocks)),
        out_specs=[vmem, vmem],
        out_shape=[shape, shape],
        scratch_shapes=[
            pltpu.VMEM(w_out.shape, BF),
            pltpu.VMEM((len(blocks) * rows, depth), BF),
            pltpu.SemaphoreType.DMA((len(blocks) + 1,)),
        ],
        compiler_params=pltpu.CompilerParams(vmem_limit_bytes=40 * 2**20),
        cost_estimate=pl.CostEstimate(
            flops=2 * len(blocks) * rows * depth * columns,
            bytes_accessed=2 * (w_out.size + len(blocks) * rows * (depth + columns)),
            transcendentals=0,
        ),
    )(places, core.reshape(1), w_out, *blocks)


def local(
    q_nope,
    q_rope,
    kv_latent,
    key_rope,
    w_uk,
    w_uv,
    w_out,
    w_gate,
    w_up,
    w_down,
    route_ids,
    route_gates,
):
    tok_rows = q_nope.shape[0]
    ctx_here = lax.axis_index("ctx")
    core = lax.axis_index("exp") % 2
    ctx_size = lax.axis_size("ctx")
    order = [ctx_at(ctx_here, dz, dy) for dz, dy in AG_ORDER]

    key_rows = jnp.concatenate([kv_latent, key_rope, key_rope], axis=1)
    half_rows = tok_rows // 2
    blocks = gather_blocks(lax.dynamic_slice_in_dim(key_rows, core * half_rows, half_rows, 0))
    pieces, starts = [key_rows], [ctx_here * tok_rows, ctx_here * tok_rows + half_rows]
    for block, source in zip(blocks[1:], order[1:], strict=True):
        pieces += [block, core_swap(block)]
        starts += [
            source * tok_rows + core * half_rows,
            source * tok_rows + (1 - core) * half_rows,
        ]
    where = jnp.stack(starts) - ctx_here * tok_rows
    places = jnp.stack(order)

    head_out = attention(where, q_nope, q_rope, pieces, w_uk, w_uv)

    mine, other = project(places, core, w_out, gather_blocks(head_out))
    pair_sum = add(mine, core_swap(other)).astype(BF)
    same_core = [[2 * i + c for i in range(8)] for c in range(2)]
    summed = lax.all_to_all(pair_sum, "exp", 0, 0, tiled=True, axis_index_groups=same_core)
    attn_out = summed.astype(F32).sum(0).astype(BF)

    out_rows = attn_out.shape[0]
    feature_cols = attn_out.shape[1]
    top_count = route_ids.shape[1]
    expert_count = lax.axis_size("exp") * w_gate.shape[0]
    capacity = 3 * out_rows * top_count // (2 * expert_count)
    slot_total = expert_count * capacity
    flat_ids = route_ids.reshape(-1)
    onehot = (flat_ids[:, None] == jnp.arange(expert_count, dtype=jnp.int32)[None, :]).astype(
        jnp.int32
    )
    earlier = jnp.cumsum(onehot, axis=0) - onehot
    slot_ids = jnp.sum(earlier * onehot, axis=1)
    targets = (flat_ids * capacity + slot_ids).reshape(out_rows, top_count)
    slot_range = jnp.arange(slot_total, dtype=jnp.int32)
    hits = targets[:, :, None] == slot_range[None, None, :]
    placing = jnp.sum(hits.astype(F32), axis=1).astype(BF).T
    weighting = jnp.sum(jnp.where(hits, route_gates[:, :, None], jnp.zeros((), BF)), axis=1)
    send_rows = jnp.dot(placing, attn_out, preferred_element_type=F32).astype(BF)
    send_rows = send_rows.reshape(expert_count, capacity, feature_cols)
    arrived = lax.all_to_all(send_rows, "exp", split_axis=0, concat_axis=0, tiled=True)
    flat_rows = arrived.reshape(slot_total, feature_cols)

    hidden_cols = w_gate.shape[2] // ctx_size

    def part(dz, dy):
        first = ctx_at(ctx_here, dz, dy) * hidden_cols
        both = jnp.concatenate(
            [lax.dynamic_slice_in_dim(w[0], first, hidden_cols, 1) for w in (w_gate, w_up)], axis=1
        )
        return jnp.dot(flat_rows, both, preferred_element_type=F32).astype(BF)

    pre = scatter_sum(part)
    hidden = (jax.nn.silu(pre[:, :hidden_cols]) * pre[:, hidden_cols:]).astype(BF)
    all_hidden = jnp.concatenate(gather_blocks(hidden), axis=1)
    down_rows = jnp.concatenate(
        [lax.dynamic_slice_in_dim(w_down[0], i * hidden_cols, hidden_cols, 0) for i in order], axis=0
    )
    expert_out = jnp.dot(all_hidden, down_rows, preferred_element_type=F32).astype(BF)
    expert_out = expert_out.reshape(expert_count, capacity, feature_cols)
    returned = lax.all_to_all(expert_out, "exp", split_axis=0, concat_axis=0, tiled=True)
    moe_out = jnp.dot(
        weighting, returned.reshape(slot_total, feature_cols), preferred_element_type=F32
    ).astype(BF)
    return (attn_out, moe_out)


def solution(mesh):
    placed = (
        P("ctx", "exp"),
        P("ctx", "exp"),
        P("ctx", None),
        P("ctx", None),
        P("exp", None, None),
        P("exp", None, None),
        P("exp", "ctx"),
        P("exp", "ctx", None),
        P("exp", "ctx", None),
        P("exp", None, "ctx"),
        P("exp", None),
        P("exp", None),
    )
    return jax.shard_map(
        local,
        mesh=mesh,
        in_specs=placed,
        out_specs=(P("exp", "ctx"), P("exp", "ctx")),
        check_vma=False,
    )
```

```python
import functools
import math

import jax
import jax.numpy as jnp
from jax import lax
from jax.experimental import pallas as pl
from jax.experimental.pallas import tpu as pltpu
from jax.sharding import PartitionSpec as P

BF = jnp.bfloat16
F32 = jnp.float32
NEG_FILL = -1e30
PIECE = 128

ZS = 4
AG_ORDER = ((0, 0), (-1, 0), (1, 0), (0, 1), (-1, 1), (1, 1), (2, 0), (2, 1))


def z_shift(array, step):
    perm = [(z * 2 + y, ((z + step) % ZS) * 2 + y) for z in range(ZS) for y in range(2)]
    return lax.ppermute(array, "ctx", perm)


def y_swap(array):
    return lax.ppermute(array, "ctx", [(i, i ^ 1) for i in range(2 * ZS)])


def x_shift(array, step):
    perm = [(x * 4 + r, ((x + step) % 4) * 4 + r) for x in range(4) for r in range(4)]
    return lax.ppermute(array, "exp", perm)


def near_swap(array):
    return lax.ppermute(array, "exp", [(e, e ^ 2) for e in range(16)])


def core_swap(array):
    return lax.ppermute(array, "exp", [(e, e ^ 1) for e in range(16)])


def ctx_at(here, dz, dy):
    z, y = here // 2, here % 2
    return ((z + dz) % ZS) * 2 + (y + dy) % 2


def first_blocks(own):
    return own, z_shift(own, 1), z_shift(own, -1), y_swap(own)


def gather_blocks(own):
    return other_blocks(first_blocks(own))


def other_blocks(blocks):
    own, up, down, side = blocks
    half = own.shape[0] // 2
    far = jnp.concatenate([z_shift(up[:half], 1), z_shift(down[half:], -1)], axis=0)
    side_up, side_down = z_shift(side, 1), z_shift(side, -1)
    return own, up, down, side, side_up, side_down, far, y_swap(far)


def add(*terms):
    return functools.reduce(jnp.add, [t.astype(F32) for t in terms])


def scatter_sum(part, shift, swap):
    got_far = swap(part(2, 1))
    got_up, got_down = shift(part(1, 1), 1), shift(part(-1, 1), -1)
    far = add(part(2, 0), got_far).astype(BF)
    half = far.shape[0] // 2
    far_up, far_down = shift(far[:half], 1), shift(far[half:], -1)
    got_side = swap(add(part(0, 1), got_up, got_down).astype(BF))
    up, down = part(1, 0), part(-1, 0)
    up = jnp.concatenate([add(up[:half], far_up).astype(BF), up[half:]], axis=0)
    down = jnp.concatenate([down[:half], add(down[half:], far_down).astype(BF)], axis=0)
    return add(part(0, 0), got_side, shift(up, 1), shift(down, -1))


def attention_kernel(where_ref, qn_ref, qr_ref, uk_ref, uv_ref, *refs, scale):
    *piece_refs, mine_ref, other_ref, keys = refs
    rows = qn_ref.shape[0]
    even = where_ref[keys.shape[0] // PIECE] == 0
    heads, nope, latent = uk_ref.shape
    vhead = uv_ref.shape[2]
    rope = qr_ref.shape[1] // heads
    factor = scale * math.log2(math.e)

    @pl.when(pl.program_id(0) == 0)
    def _():
        at = 0
        for ref in piece_refs:
            keys[at : at + ref.shape[0], :] = ref[...]
            at += ref.shape[0]

    lanes = lax.broadcasted_iota(jnp.int32, (rows, heads * rope), 1)
    ahead = lax.broadcasted_iota(jnp.int32, (rows, PIECE), 0) - lax.broadcasted_iota(
        jnp.int32, (rows, PIECE), 1
    )
    for h in range(heads):
        plain = jnp.dot(
            qn_ref[:, h * nope : (h + 1) * nope], uk_ref[h], preferred_element_type=F32
        ).astype(BF)
        mine = (lanes >= h * rope) & (lanes < (h + 1) * rope)
        turned = jnp.where(mine, qr_ref[...], jnp.zeros((), BF))
        scores = lax.dot_general(
            jnp.concatenate([plain, turned], axis=1),
            keys[...],
            (((1,), (1,)), ((), ())),
            preferred_element_type=F32,
        )
        scores = jnp.concatenate(
            [
                jnp.where(ahead >= where_ref[p], scores[:, p * PIECE : (p + 1) * PIECE], NEG_FILL)
                for p in range(keys.shape[0] // PIECE)
            ],
            axis=1,
        )
        largest = jnp.max(scores, axis=1, keepdims=True)
        terms = jnp.exp2((scores - largest) * factor)
        total = jnp.sum(terms, axis=1, keepdims=True)
        mixed = jnp.dot(terms.astype(BF), keys[:, :latent], preferred_element_type=F32)
        mixed = (mixed / total).astype(BF)
        head = jnp.dot(mixed, uv_ref[h], preferred_element_type=F32).astype(BF)
        low, high = head[: rows // 2], head[rows // 2 :]
        mine_ref[:, h * vhead : (h + 1) * vhead] = jnp.where(even, low, high)
        other_ref[:, h * vhead : (h + 1) * vhead] = jnp.where(even, high, low)


def attention(where, core, q_nope, q_rope, pieces, w_uk, w_uv):
    rows = q_nope.shape[0]
    heads, nope, latent = w_uk.shape
    vhead = w_uv.shape[2]
    rope = q_rope.shape[1] // heads
    pair = 2
    key_count = sum(p.shape[0] for p in pieces)
    width = pieces[0].shape[1]
    return pl.pallas_call(
        functools.partial(attention_kernel, scale=1.0 / math.sqrt(nope + rope)),
        grid_spec=pltpu.PrefetchScalarGridSpec(
            num_scalar_prefetch=1,
            grid=(heads // pair,),
            in_specs=[
                pl.BlockSpec((rows, pair * nope), lambda i, w: (0, i)),
                pl.BlockSpec((rows, pair * rope), lambda i, w: (0, i)),
                pl.BlockSpec((pair, nope, latent), lambda i, w: (i, 0, 0)),
                pl.BlockSpec((pair, latent, vhead), lambda i, w: (i, 0, 0)),
            ]
            + [pl.BlockSpec(p.shape, lambda i, w: (0, 0)) for p in pieces],
            out_specs=[pl.BlockSpec((rows // 2, pair * vhead), lambda i, w: (0, i))] * 2,
            scratch_shapes=[pltpu.VMEM((key_count, width), BF)],
        ),
        out_shape=[jax.ShapeDtypeStruct((rows // 2, heads * vhead), BF)] * 2,
        compiler_params=pltpu.CompilerParams(vmem_limit_bytes=60 * 2**20),
        cost_estimate=pl.CostEstimate(
            flops=2 * rows * heads * key_count * (width + latent),
            bytes_accessed=2 * (key_count * width + 2 * q_nope.size),
            transcendentals=rows * heads * key_count,
        ),
    )(jnp.append(where, core), q_nope, q_rope, w_uk, w_uv, *pieces)


def project_kernel(places_ref, *refs, depths, count, before):
    weight_refs, refs = refs[: len(depths)], refs[len(depths) :]
    block_refs, refs = refs[:count], refs[count:]
    *before_refs, out_ref, weights, blocks, sem = refs
    rows = block_refs[0].shape[0]
    copies, at = [], 0
    for ref, depth in zip(weight_refs, depths, strict=True):
        copies.append((ref, weights.at[pl.ds(at, depth)]))
        at += depth
    for n, ref in enumerate(block_refs):
        copies.append((ref, blocks.at[pl.ds(n * rows, rows)]))
    copies = [pltpu.make_async_copy(a, b, sem.at[n]) for n, (a, b) in enumerate(copies)]
    for copy in copies:
        copy.start()
    for ref in before_refs:
        for b in range(before):
            out_ref[places_ref[b]] = ref[b]
    for copy in copies:
        copy.wait()
    result = jnp.dot(blocks[...], weights[...], preferred_element_type=F32).astype(BF)
    for b in range(count):
        slot = places_ref[before + b] if before_refs else b
        out_ref[slot] = result[b * rows : (b + 1) * rows]


def project(weights, blocks, places, earlier=None):
    rows = blocks[0].shape[0]
    columns = weights[0].shape[1]
    depths = [w.shape[0] for w in weights]
    before = 0 if earlier is None else earlier.shape[0]
    vmem = pl.BlockSpec(memory_space=pltpu.VMEM)
    kernel = functools.partial(project_kernel, depths=depths, count=len(blocks), before=before)
    return pl.pallas_call(
        kernel,
        in_specs=[pl.BlockSpec(memory_space=pltpu.SMEM)]
        + [pl.BlockSpec(memory_space=pl.ANY)] * (len(weights) + len(blocks))
        + [vmem] * (before > 0),
        out_specs=vmem,
        out_shape=jax.ShapeDtypeStruct((before + len(blocks), rows, columns), BF),
        scratch_shapes=[
            pltpu.VMEM((sum(depths), columns), BF),
            pltpu.VMEM((len(blocks) * rows, sum(depths)), BF),
            pltpu.SemaphoreType.DMA((len(weights) + len(blocks),)),
        ],
        compiler_params=pltpu.CompilerParams(vmem_limit_bytes=40 * 2**20),
        cost_estimate=pl.CostEstimate(
            flops=2 * len(blocks) * rows * sum(depths) * columns,
            bytes_accessed=2 * (sum(depths) * columns + len(blocks) * rows * (sum(depths) + columns)),
            transcendentals=0,
        ),
    )(places, *weights, *blocks, *([] if earlier is None else [earlier]))


def local(
    q_nope,
    q_rope,
    kv_latent,
    key_rope,
    w_uk,
    w_uv,
    w_out,
    w_gate,
    w_up,
    w_down,
    route_ids,
    route_gates,
):
    tok_rows = q_nope.shape[0]
    ctx_here = lax.axis_index("ctx")
    core = lax.axis_index("exp") % 2
    ctx_size = lax.axis_size("ctx")
    order = [ctx_at(ctx_here, dz, dy) for dz, dy in AG_ORDER]

    key_rows = jnp.concatenate([kv_latent, key_rope, key_rope], axis=1)
    half_rows = tok_rows // 2
    blocks = gather_blocks(lax.dynamic_slice_in_dim(key_rows, core * half_rows, half_rows, 0))
    pieces, starts = [key_rows], [ctx_here * tok_rows, ctx_here * tok_rows + half_rows]
    for block, source in zip(blocks[1:], order[1:], strict=True):
        pieces += [block, core_swap(block)]
        starts += [
            source * tok_rows + core * half_rows,
            source * tok_rows + (1 - core) * half_rows,
        ]
    where = jnp.stack(starts) - ctx_here * tok_rows

    mine, other = attention(where, core, q_nope, q_rope, pieces, w_uk, w_uv)

    blocks = gather_blocks(jnp.concatenate([mine, core_swap(other)], axis=1))
    weights = [w_out, core_swap(w_out)]
    first, last = [0, 1, 2, 3, 6], [4, 5, 7]
    chip = lax.axis_index("exp") // 2
    slots = jnp.stack(
        [((order[b] // 2 - chip // 2) % 4) * 2 + (order[b] + chip) % 2 for b in first + last]
    )
    early = project(weights, [blocks[b] for b in first], slots)
    pair_sum = project(weights, [blocks[b] for b in last], slots, early)
    attn_out = scatter_sum(
        lambda step, side: pair_sum[(step % 4) * 2 + side], x_shift, near_swap
    ).astype(BF)

    out_rows = attn_out.shape[0]
    feature_cols = attn_out.shape[1]
    top_count = route_ids.shape[1]
    expert_count = lax.axis_size("exp") * w_gate.shape[0]
    capacity = 3 * out_rows * top_count // (2 * expert_count)
    slot_total = expert_count * capacity
    flat_ids = route_ids.reshape(-1)
    onehot = (flat_ids[:, None] == jnp.arange(expert_count, dtype=jnp.int32)[None, :]).astype(
        jnp.int32
    )
    earlier = jnp.cumsum(onehot, axis=0) - onehot
    slot_ids = jnp.sum(earlier * onehot, axis=1)
    targets = (flat_ids * capacity + slot_ids).reshape(out_rows, top_count)
    slot_range = jnp.arange(slot_total, dtype=jnp.int32)
    hits = targets[:, :, None] == slot_range[None, None, :]
    placing = jnp.sum(hits.astype(F32), axis=1).astype(BF).T
    weighting = jnp.sum(jnp.where(hits, route_gates[:, :, None], jnp.zeros((), BF)), axis=1)
    send_rows = jnp.dot(placing, attn_out, preferred_element_type=F32).astype(BF)
    send_rows = send_rows.reshape(expert_count, capacity, feature_cols)
    arrived = lax.all_to_all(send_rows, "exp", split_axis=0, concat_axis=0, tiled=True)
    flat_rows = arrived.reshape(slot_total, feature_cols)

    hidden_cols = w_gate.shape[2] // ctx_size

    def part(dz, dy):
        first = ctx_at(ctx_here, dz, dy) * hidden_cols
        both = jnp.concatenate(
            [lax.dynamic_slice_in_dim(w[0], first, hidden_cols, 1) for w in (w_gate, w_up)], axis=1
        )
        return jnp.dot(flat_rows, both, preferred_element_type=F32).astype(BF)

    pre = scatter_sum(part, z_shift, y_swap)
    hidden = (jax.nn.silu(pre[:, :hidden_cols]) * pre[:, hidden_cols:]).astype(BF)
    all_hidden = gather_blocks(hidden)
    expert_sum = 0.0
    for group in (first, last):
        expert_sum = expert_sum + jnp.dot(
            jnp.concatenate([all_hidden[b] for b in group], axis=1),
            jnp.concatenate(
                [
                    lax.dynamic_slice_in_dim(w_down[0], order[b] * hidden_cols, hidden_cols, 0)
                    for b in group
                ],
                axis=0,
            ),
            preferred_element_type=F32,
        )
    expert_out = expert_sum.astype(BF)
    expert_out = expert_out.reshape(expert_count, capacity, feature_cols)
    returned = lax.all_to_all(expert_out, "exp", split_axis=0, concat_axis=0, tiled=True)
    moe_out = jnp.dot(
        weighting, returned.reshape(slot_total, feature_cols), preferred_element_type=F32
    ).astype(BF)
    return (attn_out, moe_out)


def solution(mesh):
    placed = (
        P("ctx", "exp"),
        P("ctx", "exp"),
        P("ctx", None),
        P("ctx", None),
        P("exp", None, None),
        P("exp", None, None),
        P("exp", "ctx"),
        P("exp", "ctx", None),
        P("exp", "ctx", None),
        P("exp", None, "ctx"),
        P("exp", None),
        P("exp", None),
    )
    return jax.shard_map(
        local,
        mesh=mesh,
        in_specs=placed,
        out_specs=(P("exp", "ctx"), P("exp", "ctx")),
        check_vma=False,
    )
```

```python
import functools
import math

import jax
import jax.numpy as jnp
from jax import lax
from jax.experimental import pallas as pl
from jax.experimental.pallas import tpu as pltpu
from jax.sharding import PartitionSpec as P

BF = jnp.bfloat16
F32 = jnp.float32
NEG_FILL = -1e30
PIECE = 128

ZS = 4
AG_ORDER = ((0, 0), (-1, 0), (1, 0), (0, 1), (-1, 1), (1, 1), (2, 0), (2, 1))


def z_shift(array, step):
    perm = [(z * 2 + y, ((z + step) % ZS) * 2 + y) for z in range(ZS) for y in range(2)]
    return lax.ppermute(array, "ctx", perm)


def y_swap(array):
    return lax.ppermute(array, "ctx", [(i, i ^ 1) for i in range(2 * ZS)])


def x_shift(array, step):
    perm = [(x * 4 + r, ((x + step) % 4) * 4 + r) for x in range(4) for r in range(4)]
    return lax.ppermute(array, "exp", perm)


def near_swap(array):
    return lax.ppermute(array, "exp", [(e, e ^ 2) for e in range(16)])


def core_swap(array):
    return lax.ppermute(array, "exp", [(e, e ^ 1) for e in range(16)])


def ctx_at(here, dz, dy):
    z, y = here // 2, here % 2
    return ((z + dz) % ZS) * 2 + (y + dy) % 2


def first_blocks(own):
    return own, z_shift(own, 1), z_shift(own, -1), y_swap(own)


def gather_blocks(own):
    return other_blocks(first_blocks(own))


def other_blocks(blocks):
    own, up, down, side = blocks
    half = own.shape[0] // 2
    far = jnp.concatenate([z_shift(up[:half], 1), z_shift(down[half:], -1)], axis=0)
    side_up, side_down = z_shift(side, 1), z_shift(side, -1)
    return own, up, down, side, side_up, side_down, far, y_swap(far)


def add(*terms):
    return functools.reduce(jnp.add, [t.astype(F32) for t in terms])


def scatter_sum(part, shift, swap):
    got_far = swap(part(2, 1))
    got_up, got_down = shift(part(1, 1), 1), shift(part(-1, 1), -1)
    far = add(part(2, 0), got_far).astype(BF)
    half = far.shape[0] // 2
    far_up, far_down = shift(far[:half], 1), shift(far[half:], -1)
    got_side = swap(add(part(0, 1), got_up, got_down).astype(BF))
    up, down = part(1, 0), part(-1, 0)
    up = jnp.concatenate([add(up[:half], far_up).astype(BF), up[half:]], axis=0)
    down = jnp.concatenate([down[:half], add(down[half:], far_down).astype(BF)], axis=0)
    return add(part(0, 0), got_side, shift(up, 1), shift(down, -1))


def attention_kernel(where_ref, qn_ref, qr_ref, uk_ref, uv_ref, *refs, scale):
    *piece_refs, mine_ref, other_ref, keys = refs
    rows = qn_ref.shape[0]
    even = where_ref[keys.shape[0] // PIECE] == 0
    heads, nope, latent = uk_ref.shape
    vhead = uv_ref.shape[2]
    rope = qr_ref.shape[1] // heads
    factor = scale * math.log2(math.e)

    @pl.when(pl.program_id(0) == 0)
    def _():
        at = 0
        for ref in piece_refs:
            keys[at : at + ref.shape[0], :] = ref[...]
            at += ref.shape[0]

    lanes = lax.broadcasted_iota(jnp.int32, (rows, 2 * rope), 1)
    ahead = lax.broadcasted_iota(jnp.int32, (rows, PIECE), 0) - lax.broadcasted_iota(
        jnp.int32, (rows, PIECE), 1
    )

    def score(h):
        plain = jnp.dot(
            qn_ref[:, h * nope : (h + 1) * nope], uk_ref[h], preferred_element_type=F32
        ).astype(BF)
        first = h // 2 * 2 * rope
        mine = (lanes >= h % 2 * rope) & (lanes < (h % 2 + 1) * rope)
        turned = jnp.where(mine, qr_ref[:, first : first + 2 * rope], jnp.zeros((), BF))
        scores = lax.dot_general(
            jnp.concatenate([plain, turned], axis=1),
            keys[...],
            (((1,), (1,)), ((), ())),
            preferred_element_type=F32,
        )
        return jnp.concatenate(
            [
                jnp.where(ahead >= where_ref[p], scores[:, p * PIECE : (p + 1) * PIECE], NEG_FILL)
                for p in range(keys.shape[0] // PIECE)
            ],
            axis=1,
        )

    later = score(0)
    for h in range(heads):
        scores, later = later, score(h + 1) if h + 1 < heads else None
        largest = jnp.max(scores, axis=1, keepdims=True)
        terms = jnp.exp2((scores - largest) * factor)
        total = jnp.sum(terms, axis=1, keepdims=True)
        mixed = jnp.dot(terms.astype(BF), keys[:, :latent], preferred_element_type=F32)
        mixed = (mixed / total).astype(BF)
        head = jnp.dot(mixed, uv_ref[h], preferred_element_type=F32).astype(BF)
        low, high = head[: rows // 2], head[rows // 2 :]
        mine_ref[:, h * vhead : (h + 1) * vhead] = jnp.where(even, low, high)
        other_ref[:, h * vhead : (h + 1) * vhead] = jnp.where(even, high, low)


def attention(where, core, q_nope, q_rope, pieces, w_uk, w_uv):
    rows = q_nope.shape[0]
    heads, nope, latent = w_uk.shape
    vhead = w_uv.shape[2]
    rope = q_rope.shape[1] // heads
    group = 4
    key_count = sum(p.shape[0] for p in pieces)
    width = pieces[0].shape[1]
    return pl.pallas_call(
        functools.partial(attention_kernel, scale=1.0 / math.sqrt(nope + rope)),
        grid_spec=pltpu.PrefetchScalarGridSpec(
            num_scalar_prefetch=1,
            grid=(heads // group,),
            in_specs=[
                pl.BlockSpec((rows, group * nope), lambda i, w: (0, i)),
                pl.BlockSpec((rows, group * rope), lambda i, w: (0, i)),
                pl.BlockSpec((group, nope, latent), lambda i, w: (i, 0, 0)),
                pl.BlockSpec((group, latent, vhead), lambda i, w: (i, 0, 0)),
            ]
            + [pl.BlockSpec(p.shape, lambda i, w: (0, 0)) for p in pieces],
            out_specs=[pl.BlockSpec((rows // 2, group * vhead), lambda i, w: (0, i))] * 2,
            scratch_shapes=[pltpu.VMEM((key_count, width), BF)],
        ),
        out_shape=[jax.ShapeDtypeStruct((rows // 2, heads * vhead), BF)] * 2,
        compiler_params=pltpu.CompilerParams(vmem_limit_bytes=60 * 2**20),
        cost_estimate=pl.CostEstimate(
            flops=2 * rows * heads * key_count * (width + latent),
            bytes_accessed=2 * (key_count * width + 2 * q_nope.size),
            transcendentals=rows * heads * key_count,
        ),
    )(jnp.append(where, core), q_nope, q_rope, w_uk, w_uv, *pieces)


def project_kernel(places_ref, *refs, depths, count, before):
    weight_refs, refs = refs[: len(depths)], refs[len(depths) :]
    block_refs, refs = refs[:count], refs[count:]
    *before_refs, out_ref, weights, blocks, sem = refs
    rows = block_refs[0].shape[0]
    copies, at = [], 0
    for ref, depth in zip(weight_refs, depths, strict=True):
        copies.append((ref, weights.at[pl.ds(at, depth)]))
        at += depth
    for n, ref in enumerate(block_refs):
        copies.append((ref, blocks.at[pl.ds(n * rows, rows)]))
    copies = [pltpu.make_async_copy(a, b, sem.at[n]) for n, (a, b) in enumerate(copies)]
    for copy in copies:
        copy.start()
    for ref in before_refs:
        for b in range(before):
            out_ref[places_ref[b]] = ref[b]
    for copy in copies:
        copy.wait()
    result = jnp.dot(blocks[...], weights[...], preferred_element_type=F32).astype(BF)
    for b in range(count):
        slot = places_ref[before + b] if before_refs else b
        out_ref[slot] = result[b * rows : (b + 1) * rows]


def project(weights, blocks, places, earlier=None):
    rows = blocks[0].shape[0]
    columns = weights[0].shape[1]
    depths = [w.shape[0] for w in weights]
    before = 0 if earlier is None else earlier.shape[0]
    vmem = pl.BlockSpec(memory_space=pltpu.VMEM)
    kernel = functools.partial(project_kernel, depths=depths, count=len(blocks), before=before)
    return pl.pallas_call(
        kernel,
        in_specs=[pl.BlockSpec(memory_space=pltpu.SMEM)]
        + [pl.BlockSpec(memory_space=pl.ANY)] * (len(weights) + len(blocks))
        + [vmem] * (before > 0),
        out_specs=vmem,
        out_shape=jax.ShapeDtypeStruct((before + len(blocks), rows, columns), BF),
        scratch_shapes=[
            pltpu.VMEM((sum(depths), columns), BF),
            pltpu.VMEM((len(blocks) * rows, sum(depths)), BF),
            pltpu.SemaphoreType.DMA((len(weights) + len(blocks),)),
        ],
        compiler_params=pltpu.CompilerParams(vmem_limit_bytes=40 * 2**20),
        cost_estimate=pl.CostEstimate(
            flops=2 * len(blocks) * rows * sum(depths) * columns,
            bytes_accessed=2 * (sum(depths) * columns + len(blocks) * rows * (sum(depths) + columns)),
            transcendentals=0,
        ),
    )(places, *weights, *blocks, *([] if earlier is None else [earlier]))


def combine_kernel(order_ref, w_ref, *refs, count):
    block_refs, refs = refs[:count], refs[count:]
    *before_refs, out_ref, weights, blocks, sem = refs
    step = block_refs[0].shape[1]
    copies = []
    for n, ref in enumerate(block_refs):
        start = pl.multiple_of(order_ref[n] * step, step)
        source = w_ref.at[0, pl.ds(start, step)]
        copies.append((source, weights.at[pl.ds(n * step, step)]))
        copies.append((ref, blocks.at[:, pl.ds(n * step, step)]))
    copies = [pltpu.make_async_copy(a, b, sem.at[n]) for n, (a, b) in enumerate(copies)]
    for copy in copies:
        copy.start()
    for copy in copies:
        copy.wait()
    result = jnp.dot(blocks[...], weights[...], preferred_element_type=F32)
    for ref in before_refs:
        result = result + ref[...]
    out_ref[...] = result.astype(out_ref.dtype)


def combine(order, w_down, blocks, dtype, earlier=()):
    rows, step = blocks[0].shape
    columns = w_down.shape[2]
    depth = len(blocks) * step
    vmem = pl.BlockSpec(memory_space=pltpu.VMEM)
    return pl.pallas_call(
        functools.partial(combine_kernel, count=len(blocks)),
        in_specs=[pl.BlockSpec(memory_space=pltpu.SMEM)]
        + [pl.BlockSpec(memory_space=pl.ANY)] * (1 + len(blocks))
        + [vmem] * len(earlier),
        out_specs=vmem,
        out_shape=jax.ShapeDtypeStruct((rows, columns), dtype),
        scratch_shapes=[
            pltpu.VMEM((depth, columns), BF),
            pltpu.VMEM((rows, depth), BF),
            pltpu.SemaphoreType.DMA((2 * len(blocks),)),
        ],
        compiler_params=pltpu.CompilerParams(vmem_limit_bytes=40 * 2**20),
        cost_estimate=pl.CostEstimate(
            flops=2 * rows * depth * columns,
            bytes_accessed=2 * (depth * columns + rows * depth + 2 * rows * columns),
            transcendentals=0,
        ),
    )(jnp.stack(order), w_down, *blocks, *earlier)


def local(
    q_nope,
    q_rope,
    kv_latent,
    key_rope,
    w_uk,
    w_uv,
    w_out,
    w_gate,
    w_up,
    w_down,
    route_ids,
    route_gates,
):
    tok_rows = q_nope.shape[0]
    ctx_here = lax.axis_index("ctx")
    core = lax.axis_index("exp") % 2
    ctx_size = lax.axis_size("ctx")
    order = [ctx_at(ctx_here, dz, dy) for dz, dy in AG_ORDER]

    key_rows = jnp.concatenate([kv_latent, key_rope, key_rope], axis=1)
    half_rows = tok_rows // 2
    blocks = gather_blocks(lax.dynamic_slice_in_dim(key_rows, core * half_rows, half_rows, 0))
    pieces, starts = [key_rows], [ctx_here * tok_rows, ctx_here * tok_rows + half_rows]
    for block, source in zip(blocks[1:], order[1:], strict=True):
        pieces += [block, core_swap(block)]
        starts += [
            source * tok_rows + core * half_rows,
            source * tok_rows + (1 - core) * half_rows,
        ]
    where = jnp.stack(starts) - ctx_here * tok_rows

    mine, other = attention(where, core, q_nope, q_rope, pieces, w_uk, w_uv)

    blocks = gather_blocks(jnp.concatenate([mine, core_swap(other)], axis=1))
    weights = [w_out, core_swap(w_out)]
    first, last = [0, 1, 2, 3, 6], [4, 5, 7]
    chip = lax.axis_index("exp") // 2
    slots = jnp.stack(
        [((order[b] // 2 - chip // 2) % 4) * 2 + (order[b] + chip) % 2 for b in first + last]
    )
    early = project(weights, [blocks[b] for b in first], slots)
    pair_sum = project(weights, [blocks[b] for b in last], slots, early)
    attn_out = scatter_sum(
        lambda step, side: pair_sum[(step % 4) * 2 + side], x_shift, near_swap
    ).astype(BF)

    out_rows = attn_out.shape[0]
    feature_cols = attn_out.shape[1]
    top_count = route_ids.shape[1]
    expert_count = lax.axis_size("exp") * w_gate.shape[0]
    capacity = 3 * out_rows * top_count // (2 * expert_count)
    slot_total = expert_count * capacity
    flat_ids = route_ids.reshape(-1)
    onehot = (flat_ids[:, None] == jnp.arange(expert_count, dtype=jnp.int32)[None, :]).astype(
        jnp.int32
    )
    earlier = jnp.cumsum(onehot, axis=0) - onehot
    slot_ids = jnp.sum(earlier * onehot, axis=1)
    targets = (flat_ids * capacity + slot_ids).reshape(out_rows, top_count)
    slot_range = jnp.arange(slot_total, dtype=jnp.int32)
    hits = targets[:, :, None] == slot_range[None, None, :]
    placing = jnp.sum(hits.astype(F32), axis=1).astype(BF).T
    weighting = jnp.sum(jnp.where(hits, route_gates[:, :, None], jnp.zeros((), BF)), axis=1)
    send_rows = jnp.dot(placing, attn_out, preferred_element_type=F32).astype(BF)
    send_rows = send_rows.reshape(expert_count, capacity, feature_cols)
    arrived = lax.all_to_all(send_rows, "exp", split_axis=0, concat_axis=0, tiled=True)
    flat_rows = arrived.reshape(slot_total, feature_cols)

    hidden_cols = w_gate.shape[2] // ctx_size

    def part(dz, dy):
        first = ctx_at(ctx_here, dz, dy) * hidden_cols
        both = jnp.concatenate(
            [lax.dynamic_slice_in_dim(w[0], first, hidden_cols, 1) for w in (w_gate, w_up)], axis=1
        )
        return jnp.dot(flat_rows, both, preferred_element_type=F32).astype(BF)

    pre = scatter_sum(part, z_shift, y_swap)
    hidden = (jax.nn.silu(pre[:, :hidden_cols]) * pre[:, hidden_cols:]).astype(BF)
    all_hidden = gather_blocks(hidden)
    early = combine([order[b] for b in first], w_down, [all_hidden[b] for b in first], F32)
    expert_out = combine([order[b] for b in last], w_down, [all_hidden[b] for b in last], BF, [early])
    expert_out = expert_out.reshape(expert_count, capacity, feature_cols)
    returned = lax.all_to_all(expert_out, "exp", split_axis=0, concat_axis=0, tiled=True)
    moe_out = jnp.dot(
        weighting, returned.reshape(slot_total, feature_cols), preferred_element_type=F32
    ).astype(BF)
    return (attn_out, moe_out)


def solution(mesh):
    placed = (
        P("ctx", "exp"),
        P("ctx", "exp"),
        P("ctx", None),
        P("ctx", None),
        P("exp", None, None),
        P("exp", None, None),
        P("exp", "ctx"),
        P("exp", "ctx", None),
        P("exp", "ctx", None),
        P("exp", None, "ctx"),
        P("exp", None),
        P("exp", None),
    )
    return jax.shard_map(
        local,
        mesh=mesh,
        in_specs=placed,
        out_specs=(P("exp", "ctx"), P("exp", "ctx")),
        check_vma=False,
    )
```

```python
import functools
import math

import jax
import jax.numpy as jnp
from jax import lax
from jax.experimental import pallas as pl
from jax.experimental.pallas import tpu as pltpu
from jax.sharding import PartitionSpec as P

BF = jnp.bfloat16
F32 = jnp.float32
NEG_FILL = -1e30
PIECE = 128

ZS = 4
AG_ORDER = ((0, 0), (-1, 0), (1, 0), (0, 1), (-1, 1), (1, 1), (2, 0), (2, 1))


def z_shift(array, step):
    perm = [(z * 2 + y, ((z + step) % ZS) * 2 + y) for z in range(ZS) for y in range(2)]
    return lax.ppermute(array, "ctx", perm)


def y_swap(array):
    return lax.ppermute(array, "ctx", [(i, i ^ 1) for i in range(2 * ZS)])


def x_shift(array, step):
    perm = [(x * 4 + r, ((x + step) % 4) * 4 + r) for x in range(4) for r in range(4)]
    return lax.ppermute(array, "exp", perm)


def near_swap(array):
    return lax.ppermute(array, "exp", [(e, e ^ 2) for e in range(16)])


def core_swap(array):
    return lax.ppermute(array, "exp", [(e, e ^ 1) for e in range(16)])


def ctx_at(here, dz, dy):
    z, y = here // 2, here % 2
    return ((z + dz) % ZS) * 2 + (y + dy) % 2


def first_blocks(own):
    return own, z_shift(own, 1), z_shift(own, -1), y_swap(own)


def gather_blocks(own):
    own, up, down, side, side_up, side_down, far, _ = gather_parts(own)
    far = jnp.concatenate(far, axis=0)
    return own, up, down, side, side_up, side_down, far, y_swap(far)


def gather_parts(own):
    half = own.shape[0] // 2
    up, down, side = z_shift(own, 1), z_shift(own, -1), y_swap(own)
    far = z_shift(up[:half], 1), z_shift(down[half:], -1)
    side_up, side_down = z_shift(side, 1), z_shift(side, -1)
    return own, up, down, side, side_up, side_down, far, tuple(y_swap(part) for part in far)


def flat(blocks):
    return [part for block in blocks for part in (block if isinstance(block, tuple) else (block,))]


def add(*terms):
    return functools.reduce(jnp.add, [t.astype(F32) for t in terms])


def scatter_sum(part, shift, swap):
    got_far = swap(part(2, 1))
    got_up, got_down = shift(part(1, 1), 1), shift(part(-1, 1), -1)
    far = add(part(2, 0), got_far).astype(BF)
    half = far.shape[0] // 2
    far_up, far_down = shift(far[:half], 1), shift(far[half:], -1)
    got_side = swap(add(part(0, 1), got_up, got_down).astype(BF))
    up, down = part(1, 0), part(-1, 0)
    up = jnp.concatenate([add(up[:half], far_up).astype(BF), up[half:]], axis=0)
    down = jnp.concatenate([down[:half], add(down[half:], far_down).astype(BF)], axis=0)
    return add(part(0, 0), got_side, shift(up, 1), shift(down, -1))


def attention_kernel(where_ref, qn_ref, qr_ref, uk_ref, uv_ref, *refs, scale):
    *piece_refs, mine_ref, other_ref, keys = refs
    rows = qn_ref.shape[0]
    even = where_ref[keys.shape[0] // PIECE] == 0
    heads, nope, latent = uk_ref.shape
    vhead = uv_ref.shape[2]
    rope = qr_ref.shape[1] // heads
    factor = scale * math.log2(math.e)

    @pl.when(pl.program_id(0) == 0)
    def _():
        at = 0
        for ref in piece_refs:
            keys[at : at + ref.shape[0], :] = ref[...]
            at += ref.shape[0]

    lanes = lax.broadcasted_iota(jnp.int32, (rows, 2 * rope), 1)
    ahead = lax.broadcasted_iota(jnp.int32, (rows, PIECE), 0) - lax.broadcasted_iota(
        jnp.int32, (rows, PIECE), 1
    )

    def score(h):
        plain = jnp.dot(
            qn_ref[:, h * nope : (h + 1) * nope], uk_ref[h], preferred_element_type=F32
        ).astype(BF)
        first = h // 2 * 2 * rope
        mine = (lanes >= h % 2 * rope) & (lanes < (h % 2 + 1) * rope)
        turned = jnp.where(mine, qr_ref[:, first : first + 2 * rope], jnp.zeros((), BF))
        scores = lax.dot_general(
            jnp.concatenate([plain, turned], axis=1),
            keys[...],
            (((1,), (1,)), ((), ())),
            preferred_element_type=F32,
        )
        return jnp.concatenate(
            [
                jnp.where(ahead >= where_ref[p], scores[:, p * PIECE : (p + 1) * PIECE], NEG_FILL)
                for p in range(keys.shape[0] // PIECE)
            ],
            axis=1,
        )

    later = score(0)
    for h in range(heads):
        scores, later = later, score(h + 1) if h + 1 < heads else None
        largest = jnp.max(scores, axis=1, keepdims=True)
        terms = jnp.exp2((scores - largest) * factor)
        total = jnp.sum(terms, axis=1, keepdims=True)
        mixed = jnp.dot(terms.astype(BF), keys[:, :latent], preferred_element_type=F32)
        mixed = (mixed / total).astype(BF)
        head = jnp.dot(mixed, uv_ref[h], preferred_element_type=F32).astype(BF)
        low, high = head[: rows // 2], head[rows // 2 :]
        mine_ref[:, h * vhead : (h + 1) * vhead] = jnp.where(even, low, high)
        other_ref[:, h * vhead : (h + 1) * vhead] = jnp.where(even, high, low)


def attention(where, core, q_nope, q_rope, pieces, w_uk, w_uv):
    rows = q_nope.shape[0]
    heads, nope, latent = w_uk.shape
    vhead = w_uv.shape[2]
    rope = q_rope.shape[1] // heads
    group = 4
    key_count = sum(p.shape[0] for p in pieces)
    width = pieces[0].shape[1]
    return pl.pallas_call(
        functools.partial(attention_kernel, scale=1.0 / math.sqrt(nope + rope)),
        grid_spec=pltpu.PrefetchScalarGridSpec(
            num_scalar_prefetch=1,
            grid=(heads // group,),
            in_specs=[
                pl.BlockSpec((rows, group * nope), lambda i, w: (0, i)),
                pl.BlockSpec((rows, group * rope), lambda i, w: (0, i)),
                pl.BlockSpec((group, nope, latent), lambda i, w: (i, 0, 0)),
                pl.BlockSpec((group, latent, vhead), lambda i, w: (i, 0, 0)),
            ]
            + [pl.BlockSpec(p.shape, lambda i, w: (0, 0)) for p in pieces],
            out_specs=[pl.BlockSpec((rows // 2, group * vhead), lambda i, w: (0, i))] * 2,
            scratch_shapes=[pltpu.VMEM((key_count, width), BF)],
        ),
        out_shape=[jax.ShapeDtypeStruct((rows // 2, heads * vhead), BF)] * 2,
        compiler_params=pltpu.CompilerParams(vmem_limit_bytes=60 * 2**20),
        cost_estimate=pl.CostEstimate(
            flops=2 * rows * heads * key_count * (width + latent),
            bytes_accessed=2 * (key_count * width + 2 * q_nope.size),
            transcendentals=rows * heads * key_count,
        ),
    )(jnp.append(where, core), q_nope, q_rope, w_uk, w_uv, *pieces)


def project_kernel(places_ref, *refs, depths, count, parts, before):
    weight_refs, refs = refs[: len(depths)], refs[len(depths) :]
    *before_refs, out_ref, weights, blocks, sem = refs[parts:]
    block_refs = refs[:parts]
    rows = blocks.shape[0] // count
    copies, at = [], 0
    for ref, depth in zip(weight_refs, depths, strict=True):
        copies.append((ref, weights.at[pl.ds(at, depth)]))
        at += depth
    at = 0
    for ref in block_refs:
        copies.append((ref, blocks.at[pl.ds(at, ref.shape[0])]))
        at += ref.shape[0]
    copies = [pltpu.make_async_copy(a, b, sem.at[n]) for n, (a, b) in enumerate(copies)]
    for copy in copies:
        copy.start()
    for ref in before_refs:
        for b in range(before):
            out_ref[places_ref[b]] = ref[b]
    for copy in copies:
        copy.wait()
    result = jnp.dot(blocks[...], weights[...], preferred_element_type=F32).astype(BF)
    for b in range(count):
        slot = places_ref[before + b] if before_refs else b
        out_ref[slot] = result[b * rows : (b + 1) * rows]


def project(weights, blocks, places, earlier=None):
    count, blocks = len(blocks), flat(blocks)
    rows = sum(b.shape[0] for b in blocks) // count
    columns = weights[0].shape[1]
    depths = [w.shape[0] for w in weights]
    before = 0 if earlier is None else earlier.shape[0]
    vmem = pl.BlockSpec(memory_space=pltpu.VMEM)
    kernel = functools.partial(
        project_kernel, depths=depths, count=count, parts=len(blocks), before=before
    )
    return pl.pallas_call(
        kernel,
        in_specs=[pl.BlockSpec(memory_space=pltpu.SMEM)]
        + [pl.BlockSpec(memory_space=pl.ANY)] * (len(weights) + len(blocks))
        + [vmem] * (before > 0),
        out_specs=vmem,
        out_shape=jax.ShapeDtypeStruct((before + count, rows, columns), BF),
        scratch_shapes=[
            pltpu.VMEM((sum(depths), columns), BF),
            pltpu.VMEM((count * rows, sum(depths)), BF),
            pltpu.SemaphoreType.DMA((len(weights) + len(blocks),)),
        ],
        compiler_params=pltpu.CompilerParams(vmem_limit_bytes=40 * 2**20),
        cost_estimate=pl.CostEstimate(
            flops=2 * count * rows * sum(depths) * columns,
            bytes_accessed=2 * (sum(depths) * columns + count * rows * (sum(depths) + columns)),
            transcendentals=0,
        ),
    )(places, *weights, *blocks, *([] if earlier is None else [earlier]))


def combine_kernel(order_ref, w_ref, *refs, count, parts):
    *before_refs, out_ref, weights, blocks, sem = refs[parts:]
    step = refs[0].shape[1]
    copies = []
    for n in range(count):
        start = pl.multiple_of(order_ref[n] * step, step)
        source = w_ref.at[0, pl.ds(start, step)]
        copies.append((source, weights.at[pl.ds(n * step, step)]))
    at = 0
    for ref in refs[:parts]:
        n, row = at // blocks.shape[0], at % blocks.shape[0]
        copies.append((ref, blocks.at[pl.ds(row, ref.shape[0]), pl.ds(n * step, step)]))
        at += ref.shape[0]
    copies = [pltpu.make_async_copy(a, b, sem.at[n]) for n, (a, b) in enumerate(copies)]
    for copy in copies:
        copy.start()
    for copy in copies:
        copy.wait()
    result = jnp.dot(blocks[...], weights[...], preferred_element_type=F32)
    for ref in before_refs:
        result = result + ref[...]
    out_ref[...] = result.astype(out_ref.dtype)


def combine(order, w_down, blocks, dtype, earlier=()):
    count, blocks = len(blocks), flat(blocks)
    rows, step = sum(b.shape[0] for b in blocks) // count, blocks[0].shape[1]
    columns = w_down.shape[2]
    depth = count * step
    vmem = pl.BlockSpec(memory_space=pltpu.VMEM)
    return pl.pallas_call(
        functools.partial(combine_kernel, count=count, parts=len(blocks)),
        in_specs=[pl.BlockSpec(memory_space=pltpu.SMEM)]
        + [pl.BlockSpec(memory_space=pl.ANY)] * (1 + len(blocks))
        + [vmem] * len(earlier),
        out_specs=vmem,
        out_shape=jax.ShapeDtypeStruct((rows, columns), dtype),
        scratch_shapes=[
            pltpu.VMEM((depth, columns), BF),
            pltpu.VMEM((rows, depth), BF),
            pltpu.SemaphoreType.DMA((count + len(blocks),)),
        ],
        compiler_params=pltpu.CompilerParams(vmem_limit_bytes=40 * 2**20),
        cost_estimate=pl.CostEstimate(
            flops=2 * rows * depth * columns,
            bytes_accessed=2 * (depth * columns + rows * depth + 2 * rows * columns),
            transcendentals=0,
        ),
    )(jnp.stack(order), w_down, *blocks, *earlier)


def local(
    q_nope,
    q_rope,
    kv_latent,
    key_rope,
    w_uk,
    w_uv,
    w_out,
    w_gate,
    w_up,
    w_down,
    route_ids,
    route_gates,
):
    tok_rows = q_nope.shape[0]
    ctx_here = lax.axis_index("ctx")
    core = lax.axis_index("exp") % 2
    ctx_size = lax.axis_size("ctx")
    order = [ctx_at(ctx_here, dz, dy) for dz, dy in AG_ORDER]

    key_rows = jnp.concatenate([kv_latent, key_rope, key_rope], axis=1)
    half_rows = tok_rows // 2
    blocks = gather_blocks(lax.dynamic_slice_in_dim(key_rows, core * half_rows, half_rows, 0))
    pieces, starts = [key_rows], [ctx_here * tok_rows, ctx_here * tok_rows + half_rows]
    for block, source in zip(blocks[1:], order[1:], strict=True):
        pieces += [block, core_swap(block)]
        starts += [
            source * tok_rows + core * half_rows,
            source * tok_rows + (1 - core) * half_rows,
        ]
    where = jnp.stack(starts) - ctx_here * tok_rows

    mine, other = attention(where, core, q_nope, q_rope, pieces, w_uk, w_uv)

    blocks = gather_parts(jnp.concatenate([mine, core_swap(other)], axis=1))
    weights = [w_out, core_swap(w_out)]
    first, last = [0, 1, 2, 3, 6], [4, 5, 7]
    chip = lax.axis_index("exp") // 2
    slots = jnp.stack(
        [((order[b] // 2 - chip // 2) % 4) * 2 + (order[b] + chip) % 2 for b in first + last]
    )
    early = project(weights, [blocks[b] for b in first], slots)
    pair_sum = project(weights, [blocks[b] for b in last], slots, early)
    attn_out = scatter_sum(
        lambda step, side: pair_sum[(step % 4) * 2 + side], x_shift, near_swap
    ).astype(BF)

    out_rows = attn_out.shape[0]
    feature_cols = attn_out.shape[1]
    top_count = route_ids.shape[1]
    expert_count = lax.axis_size("exp") * w_gate.shape[0]
    capacity = 3 * out_rows * top_count // (2 * expert_count)
    slot_total = expert_count * capacity
    flat_ids = route_ids.reshape(-1)
    onehot = (flat_ids[:, None] == jnp.arange(expert_count, dtype=jnp.int32)[None, :]).astype(
        jnp.int32
    )
    earlier = jnp.cumsum(onehot, axis=0) - onehot
    slot_ids = jnp.sum(earlier * onehot, axis=1)
    targets = (flat_ids * capacity + slot_ids).reshape(out_rows, top_count)
    slot_range = jnp.arange(slot_total, dtype=jnp.int32)
    hits = targets[:, :, None] == slot_range[None, None, :]
    placing = jnp.sum(hits.astype(F32), axis=1).astype(BF).T
    weighting = jnp.sum(jnp.where(hits, route_gates[:, :, None], jnp.zeros((), BF)), axis=1)
    send_rows = jnp.dot(placing, attn_out, preferred_element_type=F32).astype(BF)
    send_rows = send_rows.reshape(expert_count, capacity, feature_cols)
    arrived = lax.all_to_all(send_rows, "exp", split_axis=0, concat_axis=0, tiled=True)
    flat_rows = arrived.reshape(slot_total, feature_cols)

    hidden_cols = w_gate.shape[2] // ctx_size

    def part(dz, dy):
        first = ctx_at(ctx_here, dz, dy) * hidden_cols
        both = jnp.concatenate(
            [lax.dynamic_slice_in_dim(w[0], first, hidden_cols, 1) for w in (w_gate, w_up)], axis=1
        )
        return jnp.dot(flat_rows, both, preferred_element_type=F32).astype(BF)

    pre = scatter_sum(part, z_shift, y_swap)
    hidden = (jax.nn.silu(pre[:, :hidden_cols]) * pre[:, hidden_cols:]).astype(BF)
    all_hidden = gather_parts(hidden)
    early = combine([order[b] for b in first], w_down, [all_hidden[b] for b in first], F32)
    expert_out = combine([order[b] for b in last], w_down, [all_hidden[b] for b in last], BF, [early])
    expert_out = expert_out.reshape(expert_count, capacity, feature_cols)
    returned = lax.all_to_all(expert_out, "exp", split_axis=0, concat_axis=0, tiled=True)
    moe_out = jnp.dot(
        weighting, returned.reshape(slot_total, feature_cols), preferred_element_type=F32
    ).astype(BF)
    return (attn_out, moe_out)


def solution(mesh):
    placed = (
        P("ctx", "exp"),
        P("ctx", "exp"),
        P("ctx", None),
        P("ctx", None),
        P("exp", None, None),
        P("exp", None, None),
        P("exp", "ctx"),
        P("exp", "ctx", None),
        P("exp", "ctx", None),
        P("exp", None, "ctx"),
        P("exp", None),
        P("exp", None),
    )
    return jax.shard_map(
        local,
        mesh=mesh,
        in_specs=placed,
        out_specs=(P("exp", "ctx"), P("exp", "ctx")),
        check_vma=False,
    )
```
